32 devices in a mesh: seq: 16 (over z, y, x), grp: 2 (over core).
Axes of the slice: x: 2, y: 2, z: 4, core: 2. Of those that a mesh axis runs over, the one named last changes fastest.
Arguments:
- query_rows: bfloat16 [2, 2048, 4096], P('grp', 'seq'), may hold values from -6 to 6
- key_rows: bfloat16 [2, 2048, 1024], P('grp', 'seq'), may hold values from -6 to 6
- value_rows: bfloat16 [2, 2048, 1024], P('grp', 'seq'), may hold values from -27 to 27
- doc_of_block: int32 [2, 16], P('grp'), may hold values from 0 to 3, never falling along the last dimension, each value on 1 to 8 neighbouring positions
- expert_ids: int32 [2, 2048, 2], P('grp', 'seq'), may hold values from 0 to 7, as said below
- gate_weights: float32 [2, 2048, 2], P('grp', 'seq'), may hold values from 0.1 to 0.9
- norm_gain: float32 [4096], replicated, may hold values from 0.1 to 1.9
- w_in: bfloat16 [2, 7168, 4096], P(None, ('seq', 'grp')), may hold values from -0.09375 to 0.09375
- w_down: bfloat16 [7168, 4096], P(('seq', 'grp')), may hold values from -0.0625 to 0.0625
Outputs:
- layer_out: bfloat16 [2, 2048, 4096], P('grp', 'seq')
The draws below stay inside these ranges and needn't reach their ends.
Inputs may be any that keep to these rules, and one draw needn't show every extreme that they name: `expert_ids`: each token names 2 different experts; in each aligned block of 128 tokens along a sequence (the tokens of one device) at most 40 tokens name expert 0, and in every draw some block has exactly 40 such tokens.
All inputs are finite; a program needn't handle non-finite values.
Results may differ from the reference program's by a relative error of at most 0.014.
Values may be sent and summed in bfloat16 or wider, within the bound.
A program may use at most 192 MiB of HBM per device.

```python
import math
import jax
import jax.numpy as jnp
import numpy as np
from jax import lax

D = 4096
QH = 32
KVH = 8
HD = 128
HID = 7168
EXPERTS = 8
TOP = 2
BLK = 128
TOK_DEV = 128
GROUPS = 2
LEN = 2048
NBLK = 16
DOCS = 4
DOC_MOST = 8
CAP = 40
N_SEQ = 16


def draw_query_rows(key, part):
    base = jnp.clip(jax.random.normal(jax.random.fold_in(key, 1), (GROUPS, LEN, D), jnp.float32), -6.0, 6.0)
    return base.astype(jnp.bfloat16)


def draw_key_rows(key, part):
    base = jnp.clip(jax.random.normal(jax.random.fold_in(key, 2), (GROUPS, LEN, KVH * HD), jnp.float32), -6.0, 6.0)
    return base.astype(jnp.bfloat16)


def draw_value_rows(key, part):
    column_scale = jnp.exp(jax.random.uniform(jax.random.fold_in(key, 31), (KVH * HD,), jnp.float32, math.log(0.3), math.log(3.0)))
    row_scale = jnp.exp(jax.random.uniform(jax.random.fold_in(key, 32), (GROUPS, LEN, 1), jnp.float32, math.log(0.3), math.log(3.0)))
    base = jnp.clip(jax.random.normal(jax.random.fold_in(key, 34), (GROUPS, LEN, KVH * HD), jnp.float32), -3.0, 3.0)
    return (base * column_scale * row_scale).astype(jnp.bfloat16)


def draw_expert_ids(key, part):
    nblocks = GROUPS * LEN // TOK_DEV
    counts = jax.random.randint(jax.random.fold_in(key, 41), (nblocks,), CAP // 3, CAP + 1)
    fullest = jax.random.randint(jax.random.fold_in(key, 42), (), 0, nblocks)
    counts = jnp.where(jnp.arange(nblocks) == fullest, CAP, counts)
    perm_keys = jax.random.split(jax.random.fold_in(key, 43), nblocks)
    perms = jax.vmap(lambda sub: jax.random.permutation(sub, TOK_DEV))(perm_keys)
    routed = perms < counts[:, None]
    which = jax.random.randint(jax.random.fold_in(key, 44), (nblocks, TOK_DEV), 0, 2)
    first = jax.random.randint(jax.random.fold_in(key, 45), (nblocks, TOK_DEV), 1, EXPERTS)
    offset = jax.random.randint(jax.random.fold_in(key, 46), (nblocks, TOK_DEV), 1, EXPERTS - 1)
    second = 1 + (first - 1 + offset) % (EXPERTS - 1)
    id_first = jnp.where(routed & (which == 0), 0, first)
    id_second = jnp.where(routed & (which == 1), 0, second)
    return jnp.stack([id_first, id_second], axis=-1).reshape(GROUPS, LEN, TOP).astype(jnp.int32)


def block_scale(key, shape, cuts, low, top_value):
    loudness = 1.0
    for axis_at, shards_of in cuts:
        draws = jax.random.uniform(jax.random.fold_in(jax.random.fold_in(key, 6), axis_at), (shards_of,), jnp.float32, low / len(cuts), top_value / len(cuts))
        loudness = loudness * jnp.repeat(jnp.exp(draws), shape[axis_at] // shards_of).reshape((-1,) + (1,) * (len(shape) - 1 - axis_at))
    return loudness


def length_profile(number_of, total, reach, slope):
    portions = [(1 << 20) // math.isqrt(grade ** slope) + 1 for grade in range(2, number_of + 1)]
    spare, holding = total - reach - (number_of - 1), [1] * (number_of - 1)
    while spare > 0:
        candidates = [i for i in range(number_of - 1) if holding[i] < reach]
        whole, left = sum([portions[i] for i in candidates]), spare
        for i in candidates:
            more = min(reach - holding[i], max(1, left * portions[i] // whole), spare)
            holding[i] = holding[i] + more
            spare = spare - more
    return np.array([reach] + holding)


def ragged(key, count, total, limit, skew):
    if count == 2:
        one = jax.random.randint(key, (), max(1, total - limit), min(limit, total - 1) + 1)
        return jnp.stack([one, total - one])
    tallies = jnp.asarray(length_profile(count, total, limit, skew), jnp.int32)
    pairs = (count - 1) // 2
    donor, sink = tallies[1:1 + 2 * pairs:2], tallies[2:2 + 2 * pairs:2]
    slack = jnp.minimum(donor - 1, limit - sink)
    shifted = jax.random.randint(jax.random.fold_in(key, 1), (pairs,), 0, 1 << 20) % (slack + 1)
    tallies = tallies.at[1:1 + 2 * pairs:2].set(donor - shifted).at[2:2 + 2 * pairs:2].set(sink + shifted)
    return tallies[jax.random.permutation(jax.random.fold_in(key, 2), count)]


def noise(rng, extent, width, reach, cuts=(), kind=jnp.bfloat16):
    values = jax.random.normal(rng, extent, jnp.float32) * width
    if len(cuts) > 0:
        values = block_scale(rng, extent, cuts, -0.22, 0.18) * values
    return jnp.clip(values, min=-reach, max=reach).astype(kind)


def setup_inputs(seed: int = 0) -> dict:
    keys = jax.random.split(jax.random.key(seed), 10)
    return {
        "query_rows": draw_query_rows(jax.random.fold_in(keys[9], 71), 0),
        "key_rows": draw_key_rows(jax.random.fold_in(keys[9], 71), 0),
        "value_rows": draw_value_rows(jax.random.fold_in(keys[9], 71), 0),
        "doc_of_block": jax.vmap(lambda own: jnp.searchsorted(jnp.cumsum(ragged(own, DOCS, NBLK, DOC_MOST, 2)), jnp.arange(NBLK), side="right"))(jax.random.split(keys[3], GROUPS)).reshape((GROUPS, NBLK)).astype(jnp.int32),
        "expert_ids": draw_expert_ids(jax.random.fold_in(keys[9], 71), 0),
        "gate_weights": jnp.clip(0.1 + 0.79999997 * jax.random.uniform(keys[5], (GROUPS, LEN, TOP), jnp.float32) ** block_scale(keys[5], (GROUPS, LEN, TOP), ((0, 2), (1, 16)), -0.2, 0.2), 0.1, 0.9),
        "norm_gain": jnp.clip(1.0 + 0.18 * jax.random.normal(keys[6], (D,), jnp.float32), 0.1, 1.9),
        "w_in": noise(keys[7], (2, HID, D), D ** -0.5, 0.09375, ((1, 32),)),
        "w_down": noise(keys[8], (HID, D), HID ** -0.5, 0.0625, ((0, 32),)),
    }


EPS = 1e-05
NEG = -1e+30

def attend_group(query_group, key_group, value_group, doc_group):
    token_doc = jnp.repeat(doc_group, BLK)
    allowed = token_doc[:, None] == token_doc[None, :]
    query_heads = jnp.transpose(query_group.astype(jnp.float32).reshape(LEN, QH, HD), (1, 0, 2))
    key_heads = jnp.transpose(key_group.astype(jnp.float32).reshape(LEN, KVH, HD), (1, 0, 2))
    value_heads = jnp.transpose(value_group.astype(jnp.float32).reshape(LEN, KVH, HD), (1, 0, 2))

    def one_head(head):
        query_one = query_heads[head]
        key_one = key_heads[head // 4]
        value_one = value_heads[head // 4]
        scores = jnp.dot(query_one, key_one.T, precision=lax.Precision.HIGHEST) * (1.0 / math.sqrt(HD))
        scores = jnp.where(allowed, scores, NEG)
        highest = lax.optimization_barrier(jnp.max(scores, axis=1, keepdims=True))
        weights = jnp.where(allowed, jnp.exp(scores - highest), 0.0)
        denom = lax.optimization_barrier(jnp.sum(weights, axis=1, keepdims=True))
        rounded = lax.optimization_barrier(weights.astype(jnp.bfloat16)).astype(jnp.float32)
        return jnp.dot(rounded, value_one, precision=lax.Precision.HIGHEST) / denom
    mixed = lax.map(one_head, jnp.arange(QH))
    return jnp.transpose(mixed, (1, 0, 2)).reshape(LEN, D).astype(jnp.bfloat16)

def reference(query_rows, key_rows, value_rows, doc_of_block, expert_ids, gate_weights, norm_gain, w_in, w_down):
    attended = lax.map(lambda parts: attend_group(parts[0], parts[1], parts[2], parts[3]), (query_rows, key_rows, value_rows, doc_of_block))
    attn_float = attended.astype(jnp.float32)
    spread = lax.optimization_barrier(jnp.mean(attn_float * attn_float, axis=-1, keepdims=True))
    normed = (attn_float * lax.rsqrt(spread + EPS) * norm_gain).astype(jnp.bfloat16)
    blocks = GROUPS * N_SEQ
    normed_blocks = normed.reshape(blocks, TOK_DEV, D).astype(jnp.float32)
    route_ids = expert_ids.reshape(blocks, TOK_DEV, TOP)
    chosen = route_ids == 0
    routed = jnp.any(chosen, axis=-1)
    gate_share = lax.optimization_barrier(jnp.sum(jnp.where(chosen, gate_weights.reshape(blocks, TOK_DEV, TOP), 0.0), axis=-1))
    slot_index = jnp.cumsum(routed.astype(jnp.int32), axis=1).astype(jnp.int32) - 1
    slot_ids = jnp.arange(CAP, dtype=jnp.int32)
    onehot = ((slot_index[:, None, :] == slot_ids[None, :, None]) & routed[:, None, :]).astype(jnp.float32)
    dispatched = jnp.einsum('bct,btd->bcd', onehot, normed_blocks, precision=lax.Precision.HIGHEST)
    weights_in = w_in.astype(jnp.float32)
    weights_down = w_down.astype(jnp.float32)

    def expert_rows(row_block):
        gate_up = jnp.einsum('rd,khd->krh', row_block, weights_in, precision=lax.Precision.HIGHEST)
        hidden = (jax.nn.silu(gate_up[0]) * gate_up[1]).astype(jnp.bfloat16)
        hidden = lax.optimization_barrier(hidden).astype(jnp.float32)
        return jnp.dot(hidden, weights_down, precision=lax.Precision.HIGHEST)
    results = lax.map(expert_rows, dispatched.reshape(GROUPS, N_SEQ * CAP, D))
    results = results.reshape(blocks, CAP, D)
    expert_out = jnp.einsum('bct,bcd->btd', onehot, results, precision=lax.Precision.HIGHEST)
    layer_out = attn_float.reshape(blocks, TOK_DEV, D) + gate_share[..., None] * expert_out
    return layer_out.reshape(GROUPS, LEN, D).astype(jnp.bfloat16)
```

```python
import math

import jax
import jax.numpy as jnp
from jax import lax
from jax.sharding import PartitionSpec as P

QH = 32
KVH = 8
HD = 128
BLK = 128
CAP = 40


EPS = 1e-05
NEG = -1e30


def project_in(gathered, piece):
    return jnp.einsum("rd,khd->krh", gathered, piece, preferred_element_type=jnp.float32)


def activate(gate_up):
    return (jax.nn.silu(gate_up[0]) * gate_up[1]).astype(jnp.bfloat16)


def add_down(hidden, piece):
    return jnp.dot(hidden, piece, preferred_element_type=jnp.float32)


def attend(query_all, key_all, value_all, token_doc, per_dev, kv_local):
    seq_length = query_all.shape[1]
    tile_rows = min(512, seq_length)
    tile_count = seq_length // tile_rows
    per_kv = per_dev // kv_local
    inv_root = 1.0 / math.sqrt(HD)
    query_split = query_all[0].reshape(seq_length, kv_local, per_kv, HD)
    key_split = key_all[0].reshape(seq_length, kv_local, HD)
    value_split = value_all[0].reshape(seq_length, kv_local, HD)
    outputs = []
    for q_index in range(tile_count):
        query_tile = query_split[q_index * tile_rows : (q_index + 1) * tile_rows]
        doc_query = token_doc[q_index * tile_rows : (q_index + 1) * tile_rows]
        allowed_row = doc_query[:, None] == token_doc[None, :]
        scores = (
            jnp.einsum("qkgd,tkd->kgqt", query_tile, key_split, preferred_element_type=jnp.float32)
            * inv_root
        )
        scores = jnp.where(allowed_row, scores, NEG)
        highest = jnp.max(scores, axis=3, keepdims=True)
        weights = jnp.exp(scores - highest)
        denom = jnp.sum(weights, axis=3, keepdims=True)
        mixed = jnp.einsum(
            "kgqt,tkd->qkgd",
            weights.astype(jnp.bfloat16),
            value_split,
            preferred_element_type=jnp.float32,
        )
        mixed = mixed / jnp.transpose(denom, (2, 0, 1, 3))
        outputs.append(mixed.reshape(tile_rows, per_dev * HD).astype(jnp.bfloat16))
    return jnp.concatenate(outputs, axis=0)[None]


def shards(
    query_rows,
    key_rows,
    value_rows,
    doc_of_block,
    expert_ids,
    gate_weights,
    norm_gain,
    w_in,
    w_down,
):
    seq_count = lax.axis_size("seq")
    tok_count = query_rows.shape[1]
    per_dev = QH // seq_count
    repeat_count = max(1, 4 // per_dev)
    kv_local = KVH * repeat_count // seq_count
    key_send = jnp.repeat(key_rows.reshape(1, tok_count, KVH, HD), repeat_count, axis=2).reshape(
        1, tok_count, KVH * repeat_count * HD
    )
    value_send = jnp.repeat(
        value_rows.reshape(1, tok_count, KVH, HD), repeat_count, axis=2
    ).reshape(1, tok_count, KVH * repeat_count * HD)
    query_all, key_all, value_all = (
        lax.all_to_all(query_rows, "seq", split_axis=2, concat_axis=1, tiled=True),
        lax.all_to_all(key_send, "seq", split_axis=2, concat_axis=1, tiled=True),
        lax.all_to_all(value_send, "seq", split_axis=2, concat_axis=1, tiled=True),
    )
    token_doc = jnp.repeat(doc_of_block[0], BLK)
    attended = attend(query_all, key_all, value_all, token_doc, per_dev, kv_local)
    attn_tokens = lax.all_to_all(attended, "seq", split_axis=1, concat_axis=2, tiled=True)
    attn_float = attn_tokens[0].astype(jnp.float32)
    spread = jnp.mean(attn_float * attn_float, axis=-1, keepdims=True)
    normed = (attn_float * lax.rsqrt(spread + EPS) * norm_gain).astype(jnp.bfloat16)
    chosen = expert_ids[0] == 0
    routed = jnp.any(chosen, axis=-1)
    gate_share = jnp.sum(jnp.where(chosen, gate_weights[0], 0.0), axis=-1)
    position = jnp.arange(tok_count, dtype=jnp.int32)
    earlier = (position[None, :] <= position[:, None]) & routed[None, :]
    slot_index = jnp.sum(earlier.astype(jnp.int32), axis=1) - 1
    onehot = (slot_index[None, :] == jnp.arange(CAP, dtype=jnp.int32)[:, None]) & routed[None, :]
    dispatched = jnp.dot(
        onehot.astype(jnp.bfloat16), normed, preferred_element_type=jnp.float32
    ).astype(jnp.bfloat16)
    w_in_pair = lax.all_gather(w_in, "grp", axis=1, tiled=True)
    w_down_pair = lax.all_gather(w_down, "grp", axis=0, tiled=True)
    gathered = lax.all_gather(dispatched, "seq", axis=0, tiled=True)
    gate_up = project_in(gathered, w_in_pair)
    hidden = activate(gate_up)
    terms = add_down(hidden, w_down_pair)
    returned = lax.psum_scatter(
        terms.astype(jnp.bfloat16), "seq", scatter_dimension=0, tiled=True
    )
    expert_out = lax.dot_general(
        onehot.astype(jnp.bfloat16),
        returned,
        (((0,), (0,)), ((), ())),
        preferred_element_type=jnp.float32,
    )
    layer_out = attn_float + gate_share[:, None] * expert_out
    return layer_out.astype(jnp.bfloat16)[None]


def solution(mesh):
    return jax.shard_map(
        shards,
        mesh=mesh,
        in_specs=(
            P("grp", "seq", None),
            P("grp", "seq", None),
            P("grp", "seq", None),
            P("grp", None),
            P("grp", "seq", None),
            P("grp", "seq", None),
            P(),
            P(None, ("seq", "grp"), None),
            P(("seq", "grp"), None),
        ),
        out_specs=P("grp", "seq", None),
        check_vma=False,
    )
```

```python
import functools
import math

import jax
import jax.numpy as jnp
from jax import lax
from jax.experimental import pallas as pl
from jax.experimental.pallas import tpu as pltpu
from jax.sharding import PartitionSpec as P

QH = 32
KVH = 8
HD = 128
BLK = 128
CAP = 40


DOC_MOST = 8
TEAM = 4

EPS = 1e-05
NEG = -1e30


def greet_all(n, me):
    barrier = pltpu.get_barrier_semaphore()
    for d in range(1, n):
        pl.semaphore_signal(
            barrier,
            inc=1,
            device_id={"seq": lax.rem(me + d, n)},
            device_id_type=pl.DeviceIdType.MESH,
        )
    pl.semaphore_wait(barrier, n - 1)


def greet_team(base, j):
    barrier = pltpu.get_barrier_semaphore()
    for d in range(1, TEAM):
        pl.semaphore_signal(
            barrier,
            inc=1,
            device_id={"seq": base + lax.rem(j + d, TEAM)},
            device_id_type=pl.DeviceIdType.MESH,
        )
    pl.semaphore_wait(barrier, TEAM - 1)


def span(index, size):
    return pl.ds(pl.multiple_of(index * size, size), size)


def spread_kernel(n, q_ref, k_ref, v_ref, qo_ref, ko_ref, vo_ref, *sems):
    qs, qr, ks, kr, vs, vr, own = sems
    me = lax.axis_index("seq")
    team = me // TEAM
    j = lax.rem(me, TEAM)
    tok = q_ref.shape[0]
    qw, kw = qo_ref.shape[1], ko_ref.shape[1]
    greet_all(n, me)

    def q_copy(d):
        to = lax.rem(j + d, TEAM)
        return pltpu.make_async_remote_copy(
            src_ref=q_ref.at[:, span(to, qw)],
            dst_ref=qo_ref.at[span(j, tok), :],
            send_sem=qs.at[d],
            recv_sem=qr.at[d],
            device_id={"seq": team * TEAM + to},
            device_id_type=pl.DeviceIdType.MESH,
        )

    def kv_copy(d, src, dst, send, recv):
        to = lax.rem(me + d, n)
        return pltpu.make_async_remote_copy(
            src_ref=src.at[:, span(lax.rem(to, TEAM), kw)],
            dst_ref=dst.at[span(me, tok), :],
            send_sem=send.at[d],
            recv_sem=recv.at[d],
            device_id={"seq": to},
            device_id_type=pl.DeviceIdType.MESH,
        )

    def kv_pair(d):
        return kv_copy(d, k_ref, ko_ref, ks, kr), kv_copy(d, v_ref, vo_ref, vs, vr)

    def wanted(source, team_to):
        reach = DOC_MOST - 1
        first = team_to * TEAM
        return (first - source <= reach) & (source - first <= reach + TEAM - 1)

    mine = [
        pltpu.make_async_copy(q_ref.at[:, span(j, qw)], qo_ref.at[span(j, tok), :], own.at[0]),
        pltpu.make_async_copy(k_ref.at[:, span(j, kw)], ko_ref.at[span(me, tok), :], own.at[1]),
        pltpu.make_async_copy(v_ref.at[:, span(j, kw)], vo_ref.at[span(me, tok), :], own.at[2]),
    ]
    order = sorted(range(1, n), key=lambda d: -min(d, n - d))

    def start(d):
        @pl.when(wanted(me, lax.rem(me + d, n) // TEAM))
        def _():
            for copy in kv_pair(d):
                copy.start()

    for d in order[:4]:
        start(d)
    for d in range(1, TEAM):
        q_copy(d).start()
    for d in order[4:]:
        start(d)
    for copy in mine:
        copy.start()
    for copy in mine:
        copy.wait()
    for d in range(1, TEAM):
        q_copy(d).wait()
    for d in order:

        @pl.when(wanted(me, lax.rem(me + d, n) // TEAM))
        def _():
            for copy in kv_pair(d):
                copy.wait_send()

        @pl.when(wanted(lax.rem(me - d + n, n), team))
        def _():
            for copy in kv_pair(d):
                copy.wait_recv()


def spread(n, q, k, v):
    tok = q.shape[0]
    any_spec = pl.BlockSpec(memory_space=pl.ANY)
    kv = jax.ShapeDtypeStruct((n * tok, KVH * HD // TEAM), jnp.bfloat16)
    dma = pltpu.SemaphoreType.DMA
    return pl.pallas_call(
        functools.partial(spread_kernel, n),
        out_shape=(jax.ShapeDtypeStruct((TEAM * tok, QH * HD // TEAM), jnp.bfloat16), kv, kv),
        in_specs=[any_spec] * 3,
        out_specs=(any_spec,) * 3,
        scratch_shapes=[dma((TEAM,))] * 2 + [dma((n,))] * 4 + [dma((3,))],
        compiler_params=pltpu.CompilerParams(collective_id=0, has_side_effects=True),
        name="spread",
    )(q, k, v)


def attend_kernel(start_ref, low_ref, high_ref, q_ref, k_ref, v_ref, o_ref):
    qb = pl.program_id(1)
    width = DOC_MOST * BLK
    start = start_ref[qb]
    low = (low_ref[qb] - start) * BLK
    high = (high_ref[qb] - start + 1) * BLK
    rows = pl.ds(pl.multiple_of(start * BLK, BLK), width)
    keys = k_ref[rows, :]
    row_at = lax.broadcasted_iota(jnp.int32, (width, HD), 0)
    values = v_ref[rows, :]
    values = jnp.where((row_at >= low) & (row_at < high), values, jnp.zeros_like(values))
    at = lax.broadcasted_iota(jnp.int32, (1, width), 1)
    seen = (at >= low) & (at < high)
    for h in range(QH // KVH):
        scores = lax.dot_general(
            q_ref[:, h * HD : (h + 1) * HD],
            keys,
            (((1,), (1,)), ((), ())),
            preferred_element_type=jnp.float32,
        ) * (1.0 / math.sqrt(HD))
        scores = jnp.where(seen, scores, NEG)
        weights = jnp.exp(scores - jnp.max(scores, axis=1, keepdims=True))
        denom = jnp.sum(weights, axis=1, keepdims=True)
        mixed = jnp.dot(weights.astype(jnp.bfloat16), values, preferred_element_type=jnp.float32)
        o_ref[:, h * HD : (h + 1) * HD] = (mixed / denom).astype(jnp.bfloat16)


def attend(start, low, high, q, k, v):
    kv_here = k.shape[1] // HD
    group = QH // KVH * HD
    length = k.shape[0]
    return pl.pallas_call(
        attend_kernel,
        out_shape=jax.ShapeDtypeStruct(q.shape, jnp.bfloat16),
        grid_spec=pltpu.PrefetchScalarGridSpec(
            num_scalar_prefetch=3,
            grid=(kv_here, q.shape[0] // BLK),
            in_specs=[
                pl.BlockSpec((BLK, group), lambda h, b, *_: (b, h)),
                pl.BlockSpec((length, HD), lambda h, b, *_: (0, h)),
                pl.BlockSpec((length, HD), lambda h, b, *_: (0, h)),
            ],
            out_specs=pl.BlockSpec((BLK, group), lambda h, b, *_: (b, h)),
        ),
        compiler_params=pltpu.CompilerParams(vmem_limit_bytes=40 * 2**20),
        name="attend",
    )(start, low, high, q, k, v)


def collect_kernel(a_ref, o_ref, send, recv, own):
    me = lax.axis_index("seq")
    base = me // TEAM * TEAM
    j = lax.rem(me, TEAM)
    tok, width = o_ref.shape[0], a_ref.shape[1]
    greet_team(base, j)

    def copy(d):
        to = lax.rem(j + d, TEAM)
        return pltpu.make_async_remote_copy(
            src_ref=a_ref.at[span(to, tok), :],
            dst_ref=o_ref.at[:, span(j, width)],
            send_sem=send.at[d],
            recv_sem=recv.at[d],
            device_id={"seq": base + to},
            device_id_type=pl.DeviceIdType.MESH,
        )

    for d in range(1, TEAM):
        copy(d).start()
    mine = pltpu.make_async_copy(
        a_ref.at[span(j, tok), :], o_ref.at[:, span(j, width)], own.at[0]
    )
    mine.start()
    mine.wait()
    for d in range(1, TEAM):
        copy(d).wait()


def collect(attended):
    any_spec = pl.BlockSpec(memory_space=pl.ANY)
    dma = pltpu.SemaphoreType.DMA
    return pl.pallas_call(
        collect_kernel,
        out_shape=jax.ShapeDtypeStruct((attended.shape[0] // TEAM, QH * HD), jnp.bfloat16),
        in_specs=[any_spec],
        out_specs=any_spec,
        scratch_shapes=[dma((TEAM,)), dma((TEAM,)), dma((1,))],
        compiler_params=pltpu.CompilerParams(collective_id=1, has_side_effects=True),
        name="collect",
    )(attended)


def project_in(gathered, piece):
    return jnp.einsum("rd,khd->krh", gathered, piece, preferred_element_type=jnp.float32)


def activate(gate_up):
    return (jax.nn.silu(gate_up[0]) * gate_up[1]).astype(jnp.bfloat16)


def add_down(hidden, piece):
    return jnp.dot(hidden, piece, preferred_element_type=jnp.float32)


def shards(
    query_rows,
    key_rows,
    value_rows,
    doc_of_block,
    expert_ids,
    gate_weights,
    norm_gain,
    w_in,
    w_down,
):
    seq_count = lax.axis_size("seq")
    tok_count = query_rows.shape[1]
    blocks = doc_of_block[0]
    q_all, k_all, v_all = spread(seq_count, query_rows[0], key_rows[0], value_rows[0])
    team_first = lax.axis_index("seq") // TEAM * TEAM
    team_docs = lax.dynamic_slice(blocks, (team_first,), (TEAM,))
    same = team_docs[:, None] == blocks[None, :]
    number = jnp.arange(blocks.shape[0], dtype=jnp.int32)[None, :]
    low = jnp.min(jnp.where(same, number, blocks.shape[0]), axis=1)
    high = jnp.max(jnp.where(same, number, -1), axis=1)
    first = jnp.minimum(low, blocks.shape[0] - DOC_MOST)
    attended = attend(first, low, high, q_all, k_all, v_all)
    attn_float = collect(attended).astype(jnp.float32)
    mean_square = jnp.mean(attn_float * attn_float, axis=-1, keepdims=True)
    normed = (attn_float * lax.rsqrt(mean_square + EPS) * norm_gain).astype(jnp.bfloat16)
    chosen = expert_ids[0] == 0
    routed = jnp.any(chosen, axis=-1)
    gate_share = jnp.sum(jnp.where(chosen, gate_weights[0], 0.0), axis=-1)
    position = jnp.arange(tok_count, dtype=jnp.int32)
    earlier = (position[None, :] <= position[:, None]) & routed[None, :]
    slot_index = jnp.sum(earlier.astype(jnp.int32), axis=1) - 1
    onehot = (slot_index[None, :] == jnp.arange(CAP, dtype=jnp.int32)[:, None]) & routed[None, :]
    dispatched = jnp.dot(
        onehot.astype(jnp.bfloat16), normed, preferred_element_type=jnp.float32
    ).astype(jnp.bfloat16)
    w_in_pair = lax.all_gather(w_in, "grp", axis=1, tiled=True)
    w_down_pair = lax.all_gather(w_down, "grp", axis=0, tiled=True)
    gathered = lax.all_gather(dispatched, "seq", axis=0, tiled=True)
    gate_up = project_in(gathered, w_in_pair)
    hidden = activate(gate_up)
    terms = add_down(hidden, w_down_pair)
    returned = lax.psum_scatter(
        terms.astype(jnp.bfloat16), "seq", scatter_dimension=0, tiled=True
    )
    expert_out = lax.dot_general(
        onehot.astype(jnp.bfloat16),
        returned,
        (((0,), (0,)), ((), ())),
        preferred_element_type=jnp.float32,
    )
    layer_out = attn_float + gate_share[:, None] * expert_out
    return layer_out.astype(jnp.bfloat16)[None]


def solution(mesh):
    return jax.shard_map(
        shards,
        mesh=mesh,
        in_specs=(
            P("grp", "seq", None),
            P("grp", "seq", None),
            P("grp", "seq", None),
            P("grp", None),
            P("grp", "seq", None),
            P("grp", "seq", None),
            P(),
            P(None, ("seq", "grp"), None),
            P(("seq", "grp"), None),
        ),
        out_specs=P("grp", "seq", None),
        check_vma=False,
    )
```

```python
import functools
import math

import jax
import jax.numpy as jnp
from jax import lax
from jax.experimental import pallas as pl
from jax.experimental.pallas import tpu as pltpu
from jax.sharding import PartitionSpec as P

QH = 32
KVH = 8
HD = 128
BLK = 128
CAP = 40


DOC_MOST = 8
TEAM = 4

EPS = 1e-05
NEG = -1e30


def greet_all(n, me):
    barrier = pltpu.get_barrier_semaphore()
    for d in range(1, n):
        pl.semaphore_signal(
            barrier,
            inc=1,
            device_id={"seq": lax.rem(me + d, n)},
            device_id_type=pl.DeviceIdType.MESH,
        )
    pl.semaphore_wait(barrier, n - 1)


def greet_team(base, j):
    barrier = pltpu.get_barrier_semaphore()
    for d in range(1, TEAM):
        pl.semaphore_signal(
            barrier,
            inc=1,
            device_id={"seq": base + lax.rem(j + d, TEAM)},
            device_id_type=pl.DeviceIdType.MESH,
        )
    pl.semaphore_wait(barrier, TEAM - 1)


def span(index, size):
    return pl.ds(pl.multiple_of(index * size, size), size)


def spread_kernel(n, q_ref, k_ref, v_ref, qo_ref, ko_ref, vo_ref, *sems):
    qs, qr, ks, kr, vs, vr, own = sems
    me = lax.axis_index("seq")
    team = me // TEAM
    j = lax.rem(me, TEAM)
    tok = q_ref.shape[0]
    qw, kw = qo_ref.shape[1], ko_ref.shape[1]
    greet_all(n, me)

    def q_copy(d):
        to = lax.rem(j + d, TEAM)
        return pltpu.make_async_remote_copy(
            src_ref=q_ref.at[:, span(to, qw)],
            dst_ref=qo_ref.at[span(j, tok), :],
            send_sem=qs.at[d],
            recv_sem=qr.at[d],
            device_id={"seq": team * TEAM + to},
            device_id_type=pl.DeviceIdType.MESH,
        )

    def kv_copy(d, src, dst, send, recv):
        to = lax.rem(me + d, n)
        return pltpu.make_async_remote_copy(
            src_ref=src.at[:, span(lax.rem(to, TEAM), kw)],
            dst_ref=dst.at[span(me, tok), :],
            send_sem=send.at[d],
            recv_sem=recv.at[d],
            device_id={"seq": to},
            device_id_type=pl.DeviceIdType.MESH,
        )

    def kv_pair(d):
        return kv_copy(d, k_ref, ko_ref, ks, kr), kv_copy(d, v_ref, vo_ref, vs, vr)

    def wanted(source, team_to):
        reach = DOC_MOST - 1
        first = team_to * TEAM
        return (first - source <= reach) & (source - first <= reach + TEAM - 1)

    mine = [
        pltpu.make_async_copy(q_ref.at[:, span(j, qw)], qo_ref.at[span(j, tok), :], own.at[0]),
        pltpu.make_async_copy(k_ref.at[:, span(j, kw)], ko_ref.at[span(me, tok), :], own.at[1]),
        pltpu.make_async_copy(v_ref.at[:, span(j, kw)], vo_ref.at[span(me, tok), :], own.at[2]),
    ]
    order = sorted(range(1, n), key=lambda d: -min(d, n - d))

    def start(d):
        @pl.when(wanted(me, lax.rem(me + d, n) // TEAM))
        def _():
            for copy in kv_pair(d):
                copy.start()

    for d in order[:4]:
        start(d)
    for d in range(1, TEAM):
        q_copy(d).start()
    for d in order[4:]:
        start(d)
    for copy in mine:
        copy.start()
    for copy in mine:
        copy.wait()
    for d in range(1, TEAM):
        q_copy(d).wait()
    for d in order:

        @pl.when(wanted(me, lax.rem(me + d, n) // TEAM))
        def _():
            for copy in kv_pair(d):
                copy.wait_send()

        @pl.when(wanted(lax.rem(me - d + n, n), team))
        def _():
            for copy in kv_pair(d):
                copy.wait_recv()


def spread(n, q, k, v):
    tok = q.shape[0]
    any_spec = pl.BlockSpec(memory_space=pl.ANY)
    kv = jax.ShapeDtypeStruct((n * tok, KVH * HD // TEAM), jnp.bfloat16)
    dma = pltpu.SemaphoreType.DMA
    return pl.pallas_call(
        functools.partial(spread_kernel, n),
        out_shape=(jax.ShapeDtypeStruct((TEAM * tok, QH * HD // TEAM), jnp.bfloat16), kv, kv),
        in_specs=[any_spec] * 3,
        out_specs=(any_spec,) * 3,
        scratch_shapes=[dma((TEAM,))] * 2 + [dma((n,))] * 4 + [dma((3,))],
        compiler_params=pltpu.CompilerParams(collective_id=0, has_side_effects=True),
        name="spread",
    )(q, k, v)


def attend_kernel(start_ref, low_ref, high_ref, q_ref, k_ref, v_ref, o_ref):
    qb = pl.program_id(1)
    width = DOC_MOST * BLK
    start = start_ref[qb]
    low = (low_ref[qb] - start) * BLK
    high = (high_ref[qb] - start + 1) * BLK
    rows = pl.ds(pl.multiple_of(start * BLK, BLK), width)
    keys = k_ref[rows, :]
    row_at = lax.broadcasted_iota(jnp.int32, (width, HD), 0)
    values = v_ref[rows, :]
    values = jnp.where((row_at >= low) & (row_at < high), values, jnp.zeros_like(values))
    at = lax.broadcasted_iota(jnp.int32, (1, width), 1)
    seen = (at >= low) & (at < high)
    for h in range(QH // KVH):
        scores = lax.dot_general(
            q_ref[:, h * HD : (h + 1) * HD],
            keys,
            (((1,), (1,)), ((), ())),
            preferred_element_type=jnp.float32,
        ) * (1.0 / math.sqrt(HD))
        scores = jnp.where(seen, scores, NEG)
        weights = jnp.exp(scores - jnp.max(scores, axis=1, keepdims=True))
        denom = jnp.sum(weights, axis=1, keepdims=True)
        mixed = jnp.dot(weights.astype(jnp.bfloat16), values, preferred_element_type=jnp.float32)
        o_ref[:, h * HD : (h + 1) * HD] = (mixed / denom).astype(jnp.bfloat16)


def attend(start, low, high, q, k, v):
    kv_here = k.shape[1] // HD
    group = QH // KVH * HD
    length = k.shape[0]
    return pl.pallas_call(
        attend_kernel,
        out_shape=jax.ShapeDtypeStruct(q.shape, jnp.bfloat16),
        grid_spec=pltpu.PrefetchScalarGridSpec(
            num_scalar_prefetch=3,
            grid=(kv_here, q.shape[0] // BLK),
            in_specs=[
                pl.BlockSpec((BLK, group), lambda h, b, *_: (b, h)),
                pl.BlockSpec((length, HD), lambda h, b, *_: (0, h)),
                pl.BlockSpec((length, HD), lambda h, b, *_: (0, h)),
            ],
            out_specs=pl.BlockSpec((BLK, group), lambda h, b, *_: (b, h)),
        ),
        compiler_params=pltpu.CompilerParams(vmem_limit_bytes=40 * 2**20),
        name="attend",
    )(start, low, high, q, k, v)


def collect_kernel(a_ref, o_ref, send, recv, own):
    me = lax.axis_index("seq")
    base = me // TEAM * TEAM
    j = lax.rem(me, TEAM)
    tok, width = o_ref.shape[0], a_ref.shape[1]
    greet_team(base, j)

    def copy(d):
        to = lax.rem(j + d, TEAM)
        return pltpu.make_async_remote_copy(
            src_ref=a_ref.at[span(to, tok), :],
            dst_ref=o_ref.at[:, span(j, width)],
            send_sem=send.at[d],
            recv_sem=recv.at[d],
            device_id={"seq": base + to},
            device_id_type=pl.DeviceIdType.MESH,
        )

    for d in range(1, TEAM):
        copy(d).start()
    mine = pltpu.make_async_copy(
        a_ref.at[span(j, tok), :], o_ref.at[:, span(j, width)], own.at[0]
    )
    mine.start()
    mine.wait()
    for d in range(1, TEAM):
        copy(d).wait()


def collect(attended):
    any_spec = pl.BlockSpec(memory_space=pl.ANY)
    dma = pltpu.SemaphoreType.DMA
    return pl.pallas_call(
        collect_kernel,
        out_shape=jax.ShapeDtypeStruct((attended.shape[0] // TEAM, QH * HD), jnp.bfloat16),
        in_specs=[any_spec],
        out_specs=any_spec,
        scratch_shapes=[dma((TEAM,)), dma((TEAM,)), dma((1,))],
        compiler_params=pltpu.CompilerParams(collective_id=1, has_side_effects=True),
        name="collect",
    )(attended)


def project_in(gathered, piece):
    return jnp.einsum("rd,khd->krh", gathered, piece, preferred_element_type=jnp.float32)


def activate(gate_up):
    return (jax.nn.silu(gate_up[0]) * gate_up[1]).astype(jnp.bfloat16)


def add_down(hidden, piece):
    return jnp.dot(hidden, piece, preferred_element_type=jnp.float32)


def places(n):
    me = lax.axis_index("seq")
    team, j = me // TEAM, lax.rem(me, TEAM)
    near = j + 1 - 2 * lax.rem(j, 2)
    over = j + 2 - 4 * (j // 2)
    return team, j, near, over, n // TEAM


def greet_cross(n):
    team, j, near, over, teams = places(n)
    barrier = pltpu.get_barrier_semaphore()
    others = [team * TEAM + near, team * TEAM + over]
    others += [lax.rem(team + k, teams) * TEAM + j for k in range(1, teams)]
    for other in others:
        pl.semaphore_signal(
            barrier, inc=1, device_id={"seq": other}, device_id_type=pl.DeviceIdType.MESH
        )
    pl.semaphore_wait(barrier, len(others))


def push(src, dst, send, recv, to):
    return pltpu.make_async_remote_copy(
        src_ref=src,
        dst_ref=dst,
        send_sem=send,
        recv_sem=recv,
        device_id={"seq": to},
        device_id_type=pl.DeviceIdType.MESH,
    )


def gather_kernel(n, x_ref, o_ref, cs, cr, ps, pr, own):
    team, j, near, over, teams = places(n)
    half = x_ref.shape[1] // 2
    greet_cross(n)

    def piece(k, column):
        return lax.rem(team + teams - k, teams) * TEAM + column

    def along(k):
        return push(
            x_ref,
            o_ref.at[team * TEAM + j],
            cs.at[k],
            cr.at[k],
            lax.rem(team + k, teams) * TEAM + j,
        )

    def across(k, way, to):
        index = piece(k, j)
        src = x_ref if k == 0 else o_ref.at[index]
        return push(src, o_ref.at[index], ps.at[k, way], pr.at[k, way], team * TEAM + to)

    def relay(k, way, source, part, to):
        view = o_ref.at[piece(k, source), :, pl.ds(part * half, half)]
        return push(view, view, ps.at[k, way], pr.at[k, way], team * TEAM + to)

    def fulls(k):
        return across(k, 0, near), across(k, 1, over)

    def relays(k):
        return relay(k, 2, near, 0, over), relay(k, 3, over, 1, near)

    for k in range(1, teams):
        along(k).start()
    for copy in fulls(0):
        copy.start()
    mine = pltpu.make_async_copy(x_ref, o_ref.at[team * TEAM + j], own.at[0])
    mine.start()
    for k in range(teams):
        if k + 1 < teams:
            along(k + 1).wait_recv()
            for copy in fulls(k + 1):
                copy.start()
        for full, passed in zip(fulls(k), relays(k)):
            full.wait_recv()
            passed.start()
    for k in range(teams):
        for copy in relays(k):
            copy.wait()
        for copy in fulls(k):
            copy.wait_send()
        if k:
            along(k).wait_send()
    mine.wait()


def gather_rows(n, rows):
    any_spec = pl.BlockSpec(memory_space=pl.ANY)
    dma = pltpu.SemaphoreType.DMA
    teams = n // TEAM
    return pl.pallas_call(
        functools.partial(gather_kernel, n),
        out_shape=jax.ShapeDtypeStruct((n,) + rows.shape, jnp.bfloat16),
        in_specs=[any_spec],
        out_specs=any_spec,
        scratch_shapes=[dma((teams,))] * 2 + [dma((teams, 4))] * 2 + [dma((1,))],
        compiler_params=pltpu.CompilerParams(collective_id=2, has_side_effects=True),
        name="gather_rows",
    )(rows)


def reduce_kernel(n, t_ref, o_ref, *scratch):
    far_a, far_b, add_a, add_b, from_near, from_over, plane, arrived, ps, pr, cs, cr = scratch
    team, j, near, over, teams = places(n)
    half = t_ref.shape[2] // 2
    first, second = pl.ds(0, half), pl.ds(half, half)
    f32 = jnp.float32
    greet_cross(n)

    def index(k, column):
        return lax.rem(team + k, teams) * TEAM + column

    def hop(k, way, src, dst, to):
        return push(src, dst, ps.at[k, way], pr.at[k, way], team * TEAM + to)

    def early(k):
        across = TEAM - 1 - j
        return (
            hop(k, 0, t_ref.at[index(k, across), :, first], far_a.at[k], near),
            hop(k, 1, t_ref.at[index(k, across), :, second], far_b.at[k], over),
            hop(k, 2, t_ref.at[index(k, near), :, first], from_near.at[k, 0], near),
            hop(k, 3, t_ref.at[index(k, over), :, second], from_over.at[k, 1], over),
        )

    def late(k):
        return (
            hop(k, 4, add_a.at[k], from_over.at[k, 0], over),
            hop(k, 5, add_b.at[k], from_near.at[k, 1], near),
        )

    def along(k):
        return push(plane.at[k], arrived.at[k], cs.at[k], cr.at[k], index(k, j))

    def finish(k):
        for copy in early(k)[2:] + late(k):
            copy.wait_recv()
        parts = []
        for part, cut in ((0, first), (1, second)):
            parts.append(
                t_ref[index(k, j), :, cut].astype(f32)
                + from_near[k, part].astype(f32)
                + from_over[k, part].astype(f32)
            )
        return parts

    order = list(range(teams - 1, -1, -1))
    for k in order:
        for copy in early(k):
            copy.start()
    for k in order:
        to_near, to_over = early(k)[:2]
        pass_a, pass_b = late(k)
        to_near.wait_recv()
        add_a[k] = (far_a[k].astype(f32) + t_ref[index(k, over), :, first].astype(f32)).astype(
            jnp.bfloat16
        )
        pass_a.start()
        to_over.wait_recv()
        add_b[k] = (far_b[k].astype(f32) + t_ref[index(k, near), :, second].astype(f32)).astype(
            jnp.bfloat16
        )
        pass_b.start()
        if k + 1 < teams:
            low_sum, high_sum = finish(k + 1)
            plane[k + 1, :, first] = low_sum.astype(jnp.bfloat16)
            plane[k + 1, :, second] = high_sum.astype(jnp.bfloat16)
            along(k + 1).start()
    for k in range(1, teams):
        along(k).wait()
    for cut, total in zip((first, second), finish(0)):
        for k in range(1, teams):
            total = total + arrived[k, :, cut].astype(f32)
        o_ref[:, cut] = total.astype(jnp.bfloat16)
    for k in range(teams):
        for copy in early(k) + late(k):
            copy.wait_send()


def reduce_rows(n, terms):
    dma = pltpu.SemaphoreType.DMA
    teams = n // TEAM
    rows, width = terms.shape[1:]
    halves = pltpu.VMEM((teams, rows, width // 2), jnp.bfloat16)
    pairs = pltpu.VMEM((teams, 2, rows, width // 2), jnp.bfloat16)
    wholes = pltpu.VMEM((teams, rows, width), jnp.bfloat16)
    return pl.pallas_call(
        functools.partial(reduce_kernel, n),
        out_shape=jax.ShapeDtypeStruct((rows, width), jnp.bfloat16),
        in_specs=[pl.BlockSpec(memory_space=pltpu.VMEM)],
        out_specs=pl.BlockSpec(memory_space=pltpu.VMEM),
        scratch_shapes=[halves] * 4
        + [pairs] * 2
        + [wholes] * 2
        + [dma((teams, 6))] * 2
        + [dma((teams,))] * 2,
        compiler_params=pltpu.CompilerParams(
            collective_id=3, has_side_effects=True, vmem_limit_bytes=40 * 2**20
        ),
        name="reduce_rows",
    )(terms)


def shards(
    query_rows,
    key_rows,
    value_rows,
    doc_of_block,
    expert_ids,
    gate_weights,
    norm_gain,
    w_in,
    w_down,
):
    seq_count = lax.axis_size("seq")
    tok_count = query_rows.shape[1]
    blocks = doc_of_block[0]
    q_all, k_all, v_all = spread(seq_count, query_rows[0], key_rows[0], value_rows[0])
    team_first = lax.axis_index("seq") // TEAM * TEAM
    team_docs = lax.dynamic_slice(blocks, (team_first,), (TEAM,))
    same = team_docs[:, None] == blocks[None, :]
    number = jnp.arange(blocks.shape[0], dtype=jnp.int32)[None, :]
    low = jnp.min(jnp.where(same, number, blocks.shape[0]), axis=1)
    high = jnp.max(jnp.where(same, number, -1), axis=1)
    first = jnp.minimum(low, blocks.shape[0] - DOC_MOST)
    attended = attend(first, low, high, q_all, k_all, v_all)
    attn_float = collect(attended).astype(jnp.float32)
    mean_square = jnp.mean(attn_float * attn_float, axis=-1, keepdims=True)
    normed = (attn_float * lax.rsqrt(mean_square + EPS) * norm_gain).astype(jnp.bfloat16)
    chosen = expert_ids[0] == 0
    routed = jnp.any(chosen, axis=-1)
    gate_share = jnp.sum(jnp.where(chosen, gate_weights[0], 0.0), axis=-1)
    position = jnp.arange(tok_count, dtype=jnp.int32)
    earlier = (position[None, :] <= position[:, None]) & routed[None, :]
    slot_index = jnp.sum(earlier.astype(jnp.int32), axis=1) - 1
    onehot = (slot_index[None, :] == jnp.arange(CAP, dtype=jnp.int32)[:, None]) & routed[None, :]
    dispatched = jnp.dot(
        onehot.astype(jnp.bfloat16), normed, preferred_element_type=jnp.float32
    ).astype(jnp.bfloat16)
    w_in_pair = lax.all_gather(w_in, "grp", axis=1, tiled=True)
    w_down_pair = lax.all_gather(w_down, "grp", axis=0, tiled=True)
    gathered = gather_rows(seq_count, dispatched).reshape(-1, dispatched.shape[1])
    gate_up = project_in(gathered, w_in_pair)
    hidden = activate(gate_up)
    terms = add_down(hidden, w_down_pair)
    returned = reduce_rows(
        seq_count, terms.astype(jnp.bfloat16).reshape((seq_count,) + dispatched.shape)
    )
    expert_out = lax.dot_general(
        onehot.astype(jnp.bfloat16),
        returned,
        (((0,), (0,)), ((), ())),
        preferred_element_type=jnp.float32,
    )
    layer_out = attn_float + gate_share[:, None] * expert_out
    return layer_out.astype(jnp.bfloat16)[None]


def solution(mesh):
    return jax.shard_map(
        shards,
        mesh=mesh,
        in_specs=(
            P("grp", "seq", None),
            P("grp", "seq", None),
            P("grp", "seq", None),
            P("grp", None),
            P("grp", "seq", None),
            P("grp", "seq", None),
            P(),
            P(None, ("seq", "grp"), None),
            P(("seq", "grp"), None),
        ),
        out_specs=P("grp", "seq", None),
        check_vma=False,
    )
```
